512 devices in a mesh: dp: 16 (over x_lo, z), seq: 32 (over y, x_hi, core).
Axes of the slice: x: 4 (x_hi: 2, x_lo: 2; x = x_hi * 2 + x_lo), y: 8, z: 8, core: 2. Of those that a mesh axis runs over, the one named last changes fastest.
Arguments:
- query_input: bfloat16 [65536, 4096], P(('dp', 'seq')), may hold values from -6 to 6
- key_input: bfloat16 [65536, 512], P(('dp', 'seq')), may hold values from -6 to 6
- value_input: bfloat16 [65536, 512], P(('dp', 'seq')), may hold values from -6 to 6
- output_gradient: bfloat16 [65536, 4096], P(('dp', 'seq')), may hold values from -6 to 6
Outputs:
- grad_query: bfloat16 [65536, 4096], P(('dp', 'seq'))
- grad_key: bfloat16 [65536, 512], P(('dp', 'seq'))
- grad_value: bfloat16 [65536, 512], P(('dp', 'seq'))
- query_bias_gradient: float32 [32, 128], P('seq')
- keyvalue_bias_gradient: float32 [2, 512], replicated
The draws below stay inside these ranges and needn't reach their ends.
All inputs are finite; a program needn't handle non-finite values.
Results may differ from the reference program's by a relative error of at most 0.0079.
Values may be sent and summed in bfloat16 or wider, within the bound.
A program may use at most 128 MiB of HBM per device.

```python
import math
import jax
import jax.numpy as jnp
from jax import lax

QUERY_HEADS = 32
KEYVALUE_HEADS = 4
HEAD_SIZE = 128
SEQUENCE_LENGTH = 2048
TOTAL_TOKENS = 65536


def draw_query_input(key, part):
    key = jax.random.fold_in(key, 3)
    starting_point = jax.random.truncated_normal(key, -4.0, 4.0, (TOTAL_TOKENS, QUERY_HEADS * HEAD_SIZE), jnp.float32)
    return starting_point.astype(jnp.bfloat16)


def draw_key_input(key, part):
    key = jax.random.fold_in(key, 5)
    starting_point = jax.random.truncated_normal(key, -4.0, 4.0, (TOTAL_TOKENS, KEYVALUE_HEADS * HEAD_SIZE), jnp.float32)
    return starting_point.astype(jnp.bfloat16)


def draw_output_gradient(key, part):
    key = jax.random.fold_in(key, 7)
    ramp = 0.5 + jnp.arange(TOTAL_TOKENS).astype(jnp.float32) / TOTAL_TOKENS
    starting_point = ramp[:, None] * jax.random.truncated_normal(key, -4.0, 4.0, (TOTAL_TOKENS, QUERY_HEADS * HEAD_SIZE), jnp.float32)
    return starting_point.astype(jnp.bfloat16)


def block_levels(own_key, extent, cuts, least, high):
    gain, own = 1.0, jax.random.fold_in(own_key, 6)
    for axis_at, parts in cuts:
        steps = jnp.exp(jax.random.uniform(jax.random.fold_in(own, axis_at), (parts,), jnp.float32, least / len(cuts), high / len(cuts)))
        gain = gain * jnp.repeat(steps, extent[axis_at] // parts).reshape([-1 if axis == axis_at else 1 for axis in range(len(extent))])
    return gain


def centred(rng, dims, scale, reach, shards=(), kind=jnp.bfloat16):
    values = scale * jax.random.normal(rng, dims, jnp.float32)
    if shards:
        values = values * block_levels(rng, dims, shards, -0.22, 0.18)
    return jnp.clip(values, -reach, reach).astype(kind)


def setup_inputs(seed: int = 0) -> dict:
    splits = jax.random.split(jax.random.key(seed), 5)
    return {
        "query_input": draw_query_input(jax.random.fold_in(splits[4], 71), 0),
        "key_input": draw_key_input(jax.random.fold_in(splits[4], 71), 0),
        "value_input": centred(splits[2], (TOTAL_TOKENS, KEYVALUE_HEADS * HEAD_SIZE), 1.0, 6.0, ((0, 512),)),
        "output_gradient": draw_output_gradient(jax.random.fold_in(splits[4], 71), 0),
    }


def one_sequence(portions):
    query_row_block, key_row_block, value_row_block, gradient_rows = portions
    span_length = query_row_block.shape[0]
    group_width = QUERY_HEADS // KEYVALUE_HEADS
    scaling = 1.0 / math.sqrt(HEAD_SIZE)
    query_float = query_row_block.reshape(span_length, KEYVALUE_HEADS, group_width, HEAD_SIZE).astype(jnp.float32)
    gradient_float = gradient_rows.reshape(span_length, KEYVALUE_HEADS, group_width, HEAD_SIZE).astype(jnp.float32)
    key_float = key_row_block.reshape(span_length, KEYVALUE_HEADS, HEAD_SIZE).astype(jnp.float32)
    value_float = value_row_block.reshape(span_length, KEYVALUE_HEADS, HEAD_SIZE).astype(jnp.float32)
    scores = jnp.einsum('qkgd,tkd->kgqt', query_float, key_float) * scaling
    row_ids = lax.broadcasted_iota(jnp.int32, (span_length, span_length), 0)
    col_ids = lax.broadcasted_iota(jnp.int32, (span_length, span_length), 1)
    scores = jnp.where(col_ids <= row_ids, scores, -jnp.inf)
    peak = lax.optimization_barrier(jnp.max(scores, axis=3, keepdims=True))
    log_total = peak + jnp.log(lax.optimization_barrier(jnp.sum(jnp.exp(scores - peak), axis=3, keepdims=True)))
    probs = jnp.exp(scores - log_total)
    probs_half = lax.optimization_barrier(probs.astype(jnp.bfloat16)).astype(jnp.float32)
    output = jnp.einsum('kgqt,tkd->qkgd', probs_half, value_float)
    delta = lax.optimization_barrier(jnp.sum(gradient_float * output, axis=3)).transpose(1, 2, 0)
    value_gradient_total = jnp.einsum('jpox,ojpa->xja', probs_half, gradient_float)
    dprobs = jnp.einsum('qkgd,tkd->kgqt', gradient_float, value_float)
    dscores = probs * (dprobs - delta[..., None]) * scaling
    score_gradient_half = lax.optimization_barrier(dscores.astype(jnp.bfloat16)).astype(jnp.float32)
    query_grad = jnp.einsum('kgqt,tkd->qkgd', score_gradient_half, key_float).reshape(span_length, QUERY_HEADS * HEAD_SIZE)
    key_gradient_total = jnp.einsum('jpox,ojpa->xja', score_gradient_half, query_float).reshape(span_length, KEYVALUE_HEADS * HEAD_SIZE)
    value_gradient_total = value_gradient_total.reshape(span_length, KEYVALUE_HEADS * HEAD_SIZE)
    return (query_grad.astype(jnp.bfloat16), key_gradient_total.astype(jnp.bfloat16), value_gradient_total.astype(jnp.bfloat16), lax.optimization_barrier(jnp.sum(query_grad, axis=0)), lax.optimization_barrier(jnp.sum(key_gradient_total, axis=0)), lax.optimization_barrier(jnp.sum(value_gradient_total, axis=0)))

def reference(query_input, key_input, value_input, output_gradient):
    item_count = TOTAL_TOKENS // SEQUENCE_LENGTH
    portions = (query_input.reshape(item_count, SEQUENCE_LENGTH, QUERY_HEADS * HEAD_SIZE), key_input.reshape(item_count, SEQUENCE_LENGTH, KEYVALUE_HEADS * HEAD_SIZE), value_input.reshape(item_count, SEQUENCE_LENGTH, KEYVALUE_HEADS * HEAD_SIZE), output_gradient.reshape(item_count, SEQUENCE_LENGTH, QUERY_HEADS * HEAD_SIZE))
    query_gradient, key_gradient, value_gradient, sum_q, sum_k, sum_v = lax.map(one_sequence, portions)
    root_norm = 1.0 / math.sqrt(TOTAL_TOKENS)
    query_bias_gradient = (lax.optimization_barrier(jnp.sum(sum_q, axis=0)) * root_norm).reshape(QUERY_HEADS, HEAD_SIZE)
    keyvalue_bias_gradient = jnp.stack([lax.optimization_barrier(jnp.sum(sum_k, axis=0)), lax.optimization_barrier(jnp.sum(sum_v, axis=0))]) * root_norm
    return (query_gradient.reshape(TOTAL_TOKENS, QUERY_HEADS * HEAD_SIZE), key_gradient.reshape(TOTAL_TOKENS, KEYVALUE_HEADS * HEAD_SIZE), value_gradient.reshape(TOTAL_TOKENS, KEYVALUE_HEADS * HEAD_SIZE), query_bias_gradient, keyvalue_bias_gradient)
```

```python
import functools
import math

import jax
import jax.numpy as jnp
from jax import lax
from jax.experimental import pallas as pl
from jax.experimental.pallas import tpu as pltpu
from jax.sharding import PartitionSpec as P

QUERY_HEADS = 32
KEYVALUE_HEADS = 4
HEAD_SIZE = 128
GROUP = QUERY_HEADS // KEYVALUE_HEADS
ROWS = 128
BLOCK = 256
CHUNKS = 8
SPAN = BLOCK * CHUNKS
HALF = 16
SLOTS = 3
FAR = 6
COLS = GROUP * HEAD_SIZE
SCALE = 1.0 / math.sqrt(HEAD_SIZE)
SCALE2 = SCALE * math.log2(math.e)

F32 = jnp.float32
BF16 = jnp.bfloat16
MESH = pl.DeviceIdType.MESH
NT = (((1,), (1,)), ((), ()))
NN = (((1,), (0,)), ((), ()))
TN = (((0,), (0,)), ((), ()))


def dot(a, b, dims):
    return lax.dot_general(a, b, dims, preferred_element_type=F32)


def fold(x, op):
    return op(x.reshape(x.shape[0] // 8, 8, x.shape[1]), axis=0)


def at(start, size):
    return pl.ds(pl.multiple_of(start, size), size)


def host(half, chunk, side, core):
    far = chunk // FAR if side else 0
    device = ((half + far) % 2) * HALF + (chunk - FAR * far) * 2 + core
    return device, side + far


def send(src, dst, send_sem, recv_sem, device, me):
    @pl.when(device != me)
    def _():
        pltpu.make_async_remote_copy(
            src, dst, send_sem, recv_sem, device_id={"seq": device}, device_id_type=MESH
        ).start()

    @pl.when(device == me)
    def _():
        pltpu.make_async_copy(src, dst, recv_sem).start()


def sent(src, dst, send_sem, recv_sem, device, me):
    @pl.when(device != me)
    def _():
        pltpu.make_async_remote_copy(
            src, dst, send_sem, recv_sem, device_id={"seq": device}, device_id_type=MESH
        ).wait_send()


def landed(ref, sem):
    pltpu.make_async_copy(ref, ref, sem).wait()


def main_kernel(
    q_in, k_in, v_in, g_in,
    dq_out, dk_out, dv_out, qb_out, kvb_out,
    qs, gs, ks, vs, scores, dprobs, dqs, dkst, dvst, dqst, rk, rv, qb, kvb, rqb, rkvb,
    q_send, q_recv, k_send, k_recv, d_send, d_recv, dq_send, dq_recv, b_send, b_recv, kvb_send, kvb_recv,
):
    me = lax.axis_index("seq")
    half = me // HALF
    index = me % HALF
    chunk = index // 2
    core = index % 2

    barrier = pltpu.get_barrier_semaphore()

    def greet(step, carry):
        other = (me + step) % (2 * HALF)
        pl.semaphore_signal(barrier, inc=1, device_id={"seq": other}, device_id_type=MESH)
        return carry

    lax.fori_loop(1, 2 * HALF, greet, 0)
    pl.semaphore_wait(barrier, 2 * HALF - 1)

    def spread(act):
        for side in range(2):
            for part in range(2):
                rows_in, rows_at = ((q_in, qs), (g_in, gs))[part]
                keys_in, keys_at = ((k_in, ks), (v_in, vs))[part]
                for to in range(2):
                    head = 2 * to + side
                    device, slot = host(half, chunk, side, to)
                    act(
                        rows_in.at[:, pl.ds(head * COLS, COLS)],
                        rows_at.at[slot, at(core * ROWS, ROWS)],
                        q_send.at[head, part],
                        q_recv.at[slot, part],
                        device,
                        me,
                    )

                def step(i, carry):
                    later = CHUNKS - 1 - i
                    for to in range(2):
                        head = 2 * to + side
                        device, slot = host(half, later, side, to)
                        act(
                            keys_in.at[:, pl.ds(head * HEAD_SIZE, HEAD_SIZE)],
                            keys_at.at[slot, at(index * ROWS, ROWS)],
                            k_send.at[later, head, part],
                            k_recv.at[slot, chunk, part],
                            device,
                            me,
                        )
                    return carry

                lax.fori_loop(0, CHUNKS - chunk, step, 0)

    spread(send)

    key_ids = lax.broadcasted_iota(jnp.int32, (BLOCK, BLOCK), 0)
    query_ids = lax.broadcasted_iota(jnp.int32, (BLOCK, BLOCK), 1)
    cols = [pl.ds(j * HEAD_SIZE, HEAD_SIZE) for j in range(GROUP)]

    def where_job(slot):
        far = slot // 2
        return (half + far) % 2, chunk + FAR * far, 2 * core + (slot + 1) // 2

    def back(act, slot, block):
        job_half, job_chunk, head = where_job(slot)
        for part in range(2):
            stage, place = ((dkst, rk), (dvst, rv))[part]
            for to in range(2):
                act(
                    stage.at[slot, at(block * BLOCK + to * ROWS, ROWS)],
                    place.at[job_chunk, :, at(head * HEAD_SIZE, HEAD_SIZE)],
                    d_send.at[slot, block, to, part],
                    d_recv.at[job_chunk, part],
                    job_half * HALF + block * 2 + to,
                    me,
                )

    def back_rows(act, slot):
        job_half, job_chunk, head = where_job(slot)
        for to in range(2):
            act(
                dqst.at[slot, pl.ds(to * ROWS, ROWS)],
                dq_out.at[:, at(head * COLS, COLS)],
                dq_send.at[slot, to],
                dq_recv,
                job_half * HALF + job_chunk * 2 + to,
                me,
            )

    def back_bias(act, slot):
        job_half, job_chunk, head = where_job(slot)
        source = job_half * CHUNKS + job_chunk
        act(kvb.at[slot], rkvb.at[source], kvb_send.at[slot], kvb_recv, head * GROUP, me)
        for j in range(GROUP):
            act(
                qb.at[slot * GROUP + j],
                rqb.at[source],
                b_send.at[slot, j],
                b_recv,
                head * GROUP + j,
                me,
            )

    def job(slot, carry):
        _, job_chunk, _ = where_job(slot)

        def pass_scores(block, peaks, diagonal):
            landed(ks.at[slot, at(block * BLOCK, BLOCK)], k_recv.at[slot, block, 0])
            rows = at(block * BLOCK, BLOCK)
            key_block = ks[slot, rows, :]
            out = []
            for j in range(GROUP):
                s = dot(key_block, qs[slot, :, cols[j]], NT)
                if diagonal:
                    s = jnp.where(key_ids <= query_ids, s, -jnp.inf)
                scores[j, rows, :] = s
                out.append(jnp.maximum(peaks[j], fold(s, jnp.max)))
            return tuple(out)

        landed(qs.at[slot], q_recv.at[slot, 0])
        peaks = tuple(jnp.full((8, BLOCK), -jnp.inf, F32) for _ in range(GROUP))
        peaks = pass_scores(job_chunk, peaks, True)
        peaks = lax.fori_loop(
            0, job_chunk, lambda i, c: pass_scores(job_chunk - 1 - i, c, False), peaks
        )
        peaks = [jnp.max(x, axis=0, keepdims=True) * SCALE2 for x in peaks]

        def pass_probs(i, sums):
            block = job_chunk - i
            landed(vs.at[slot, at(block * BLOCK, BLOCK)], k_recv.at[slot, block, 1])
            rows = at(block * BLOCK, BLOCK)
            value_block = vs[slot, rows, :]
            out = []
            for j in range(GROUP):
                p = jnp.exp2(scores[j, rows, :] * SCALE2 - peaks[j])
                dp = dot(value_block, gs[slot, :, cols[j]], NT)
                scores[j, rows, :] = p
                dprobs[j, rows, :] = dp
                out.append((sums[j][0] + fold(p, jnp.sum), sums[j][1] + fold(p * dp, jnp.sum)))
            return tuple(out)

        landed(gs.at[slot], q_recv.at[slot, 1])
        zero = jnp.zeros((8, BLOCK), F32)
        sums = lax.fori_loop(
            0, job_chunk + 1, pass_probs, tuple((zero, zero) for _ in range(GROUP))
        )
        inverse = [1.0 / jnp.sum(x[0], axis=0, keepdims=True) for x in sums]
        delta = [jnp.sum(x[1], axis=0, keepdims=True) * r for x, r in zip(sums, inverse)]

        dqs[...] = jnp.zeros_like(dqs)

        def pass_grads(i, bias):
            block = job_chunk - i
            rows = at(block * BLOCK, BLOCK)
            key_block = ks[slot, rows, :]
            dv = jnp.zeros((BLOCK, HEAD_SIZE), F32)
            dk = jnp.zeros((BLOCK, HEAD_SIZE), F32)
            for j in range(GROUP):
                p = scores[j, rows, :] * inverse[j]
                ds = (p * (dprobs[j, rows, :] - delta[j])).astype(BF16)
                dv = dv + dot(p.astype(BF16), gs[slot, :, cols[j]], NN)
                dk = dk + dot(ds, qs[slot, :, cols[j]], NN)
                dqs[:, cols[j]] += dot(ds, key_block, TN)
            dk = dk * SCALE
            dkst[slot, rows, :] = dk.astype(BF16)
            dvst[slot, rows, :] = dv.astype(BF16)
            back(send, slot, block)
            return bias[0] + fold(dk, jnp.sum), bias[1] + fold(dv, jnp.sum)

        zero = jnp.zeros((8, HEAD_SIZE), F32)
        bias = lax.fori_loop(0, job_chunk + 1, pass_grads, (zero, zero))
        for part in range(2):
            kvb[slot, pl.ds(part, 1), :] = jnp.sum(bias[part], axis=0, keepdims=True)
        for j in range(GROUP):
            x = dqs[:, cols[j]] * SCALE
            dqst[slot, :, cols[j]] = x.astype(BF16)
            qb[slot * GROUP + j] = jnp.sum(fold(x, jnp.sum), axis=0, keepdims=True)
        back_bias(send, slot)
        back_rows(send, slot)
        return carry

    jobs = SLOTS - (chunk + 2) // 4
    lax.fori_loop(0, jobs, job, 0)

    landed(rqb, b_recv)
    qb_out[...] = jnp.sum(rqb[...], axis=0)

    @pl.when(me % GROUP == 0)
    def _():
        landed(rkvb, kvb_recv)
        kvb_out[...] = jnp.sum(rkvb[...], axis=0)

    @pl.when(me % GROUP != 0)
    def _():
        kvb_out[...] = jnp.zeros_like(kvb_out)

    for part in range(2):
        place, out = ((rk, dk_out), (rv, dv_out))[part]

        def gather(later, total):
            landed(place.at[later], d_recv.at[later, part])
            return total + place[later].astype(F32)

        total = jnp.zeros((ROWS, KEYVALUE_HEADS * HEAD_SIZE), F32)
        out[...] = lax.fori_loop(chunk, CHUNKS, gather, total).astype(BF16)

    landed(dq_out, dq_recv)

    spread(sent)

    def close(slot, carry):
        _, job_chunk, _ = where_job(slot)

        def step(block, c):
            back(sent, slot, block)
            return c

        lax.fori_loop(0, job_chunk + 1, step, 0)
        back_bias(sent, slot)
        back_rows(sent, slot)
        return carry

    lax.fori_loop(0, jobs, close, 0)


def bias_kernel(groups, norm, qb_in, kvb_in, qb_out, kvb_out, mine, theirs, kv, all_kv,
                x_send, x_recv, y_send, y_recv):
    me = lax.axis_index("seq")
    group = lax.axis_index("dp")
    members = 2 * HALF
    barrier = pltpu.get_barrier_semaphore()

    def greet_group(step, carry):
        other = (group + step) % groups
        pl.semaphore_signal(barrier, inc=1, device_id={"dp": other}, device_id_type=MESH)
        return carry

    def greet(step, carry):
        other = (me + step) % members
        pl.semaphore_signal(barrier, inc=1, device_id={"seq": other}, device_id_type=MESH)
        return carry

    lax.fori_loop(1, groups, greet_group, 0)
    lax.fori_loop(1, members, greet, 0)
    mine[pl.ds(0, 1), :] = qb_in[...]
    mine[pl.ds(1, 2), :] = kvb_in[...]
    mine[pl.ds(3, 5), :] = jnp.zeros((5, HEAD_SIZE), F32)
    pl.semaphore_wait(barrier, groups - 1 + members - 1)

    def across(step):
        return pltpu.make_async_remote_copy(
            mine, theirs.at[step - 1], x_send.at[step - 1], x_recv,
            device_id={"dp": (group + step) % groups}, device_id_type=MESH,
        )

    def start(step, carry):
        across(step).start()
        return carry

    lax.fori_loop(1, groups, start, 0)
    landed(theirs, x_recv)
    total = (mine[...] + jnp.sum(theirs[...], axis=0)) * norm
    qb_out[...] = total[0:1]
    kv[...] = total[1:3]

    def along(step):
        return pltpu.make_async_remote_copy(
            kv, all_kv.at[me // GROUP], y_send.at[step - 1], y_recv,
            device_id={"seq": (me + step) % members}, device_id_type=MESH,
        )

    @pl.when(me % GROUP == 0)
    def _():
        def start(step, carry):
            along(step).start()
            return carry

        lax.fori_loop(1, members, start, 0)
        pltpu.make_async_copy(kv, all_kv.at[me // GROUP], y_recv).start()

    landed(all_kv, y_recv)
    for head in range(KEYVALUE_HEADS):
        kvb_out[:, pl.ds(head * HEAD_SIZE, HEAD_SIZE)] = all_kv[head]

    def finish(step, carry):
        across(step).wait_send()
        return carry

    lax.fori_loop(1, groups, finish, 0)

    @pl.when(me % GROUP == 0)
    def _():
        def finish(step, carry):
            along(step).wait_send()
            return carry

        lax.fori_loop(1, members, finish, 0)


def local(query_input, key_input, value_input, output_gradient):
    groups = lax.axis_size("dp")
    vmem = pl.BlockSpec(memory_space=pltpu.VMEM)
    any_space = pl.BlockSpec(memory_space=pl.ANY)
    dma = pltpu.SemaphoreType.DMA
    kv_cols = KEYVALUE_HEADS * HEAD_SIZE
    grad_query, grad_key, grad_value, query_sum, keyvalue_sum = pl.pallas_call(
        main_kernel,
        out_shape=[
            jax.ShapeDtypeStruct((ROWS, QUERY_HEADS * HEAD_SIZE), BF16),
            jax.ShapeDtypeStruct((ROWS, kv_cols), BF16),
            jax.ShapeDtypeStruct((ROWS, kv_cols), BF16),
            jax.ShapeDtypeStruct((1, HEAD_SIZE), F32),
            jax.ShapeDtypeStruct((2, HEAD_SIZE), F32),
        ],
        in_specs=[any_space] * 4,
        out_specs=[any_space, vmem, vmem, vmem, vmem],
        scratch_shapes=[
            pltpu.VMEM((SLOTS, BLOCK, COLS), BF16),
            pltpu.VMEM((SLOTS, BLOCK, COLS), BF16),
            pltpu.VMEM((SLOTS, SPAN, HEAD_SIZE), BF16),
            pltpu.VMEM((SLOTS, SPAN, HEAD_SIZE), BF16),
            pltpu.VMEM((GROUP, SPAN, BLOCK), F32),
            pltpu.VMEM((GROUP, SPAN, BLOCK), F32),
            pltpu.VMEM((BLOCK, COLS), F32),
            pltpu.VMEM((SLOTS, SPAN, HEAD_SIZE), BF16),
            pltpu.VMEM((SLOTS, SPAN, HEAD_SIZE), BF16),
            pltpu.VMEM((SLOTS, BLOCK, COLS), BF16),
            pltpu.VMEM((CHUNKS, ROWS, kv_cols), BF16),
            pltpu.VMEM((CHUNKS, ROWS, kv_cols), BF16),
            pltpu.VMEM((SLOTS * GROUP, 1, HEAD_SIZE), F32),
            pltpu.VMEM((SLOTS, 2, HEAD_SIZE), F32),
            pltpu.VMEM((2 * CHUNKS, 1, HEAD_SIZE), F32),
            pltpu.VMEM((2 * CHUNKS, 2, HEAD_SIZE), F32),
            dma((KEYVALUE_HEADS, 2)),
            dma((SLOTS, 2)),
            dma((CHUNKS, KEYVALUE_HEADS, 2)),
            dma((SLOTS, CHUNKS, 2)),
            dma((SLOTS, CHUNKS, 2, 2)),
            dma((CHUNKS, 2)),
            dma((SLOTS, 2)),
            dma,
            dma((SLOTS, GROUP)),
            dma,
            dma((SLOTS,)),
            dma,
        ],
        compiler_params=pltpu.CompilerParams(
            collective_id=0, has_side_effects=True, vmem_limit_bytes=60 * 2**20
        ),
        name="attention_grads",
    )(query_input, key_input, value_input, output_gradient)
    norm = 1.0 / math.sqrt(ROWS * 2 * HALF * groups)
    query_bias, keyvalue_bias = pl.pallas_call(
        functools.partial(bias_kernel, groups, norm),
        out_shape=[
            jax.ShapeDtypeStruct((1, HEAD_SIZE), F32),
            jax.ShapeDtypeStruct((2, kv_cols), F32),
        ],
        in_specs=[vmem] * 2,
        out_specs=[vmem] * 2,
        scratch_shapes=[
            pltpu.VMEM((8, HEAD_SIZE), F32),
            pltpu.VMEM((groups - 1, 8, HEAD_SIZE), F32),
            pltpu.VMEM((2, HEAD_SIZE), F32),
            pltpu.VMEM((KEYVALUE_HEADS, 2, HEAD_SIZE), F32),
            dma((groups - 1,)),
            dma,
            dma((2 * HALF - 1,)),
            dma,
        ],
        compiler_params=pltpu.CompilerParams(collective_id=1, has_side_effects=True),
        name="bias_sums",
    )(query_sum, keyvalue_sum)
    return grad_query, grad_key, grad_value, query_bias, keyvalue_bias


def solution(mesh):
    rows = P(("dp", "seq"), None)
    return jax.shard_map(
        local,
        mesh=mesh,
        in_specs=(rows,) * 4,
        out_specs=(rows, rows, rows, P("seq", None), P()),
        check_vma=False,
    )
```

```python
import functools
import math

import jax
import jax.numpy as jnp
from jax import lax
from jax.experimental import pallas as pl
from jax.experimental.pallas import tpu as pltpu
from jax.sharding import PartitionSpec as P

QUERY_HEADS = 32
KEYVALUE_HEADS = 4
HEAD_SIZE = 128
GROUP = QUERY_HEADS // KEYVALUE_HEADS
ROWS = 128
BLOCK = 256
CHUNKS = 8
SPAN = BLOCK * CHUNKS
HALF = 16
SLOTS = 2
LINE = 4
COLS = GROUP * HEAD_SIZE
SCALE = 1.0 / math.sqrt(HEAD_SIZE)
SCALE2 = SCALE * math.log2(math.e)

F32 = jnp.float32
BF16 = jnp.bfloat16
MESH = pl.DeviceIdType.MESH
NT = (((1,), (1,)), ((), ()))
NN = (((1,), (0,)), ((), ()))
TN = (((0,), (0,)), ((), ()))


def dot(a, b, dims):
    return lax.dot_general(a, b, dims, preferred_element_type=F32)


def fold(x, op):
    return op(x.reshape(x.shape[0] // 8, 8, x.shape[1]), axis=0)


def at(start, size):
    return pl.ds(pl.multiple_of(start, size), size)


def remote(src, dst, send_sem, recv_sem, device):
    return pltpu.make_async_remote_copy(
        src, dst, send_sem, recv_sem, device_id=device, device_id_type=MESH
    )


def send(src, dst, send_sem, recv_sem, device, me):
    @pl.when(device != me)
    def _():
        remote(src, dst, send_sem, recv_sem, {"seq": device}).start()

    @pl.when(device == me)
    def _():
        pltpu.make_async_copy(src, dst, recv_sem).start()


def sent(src, dst, send_sem, recv_sem, device, me):
    @pl.when(device != me)
    def _():
        remote(src, dst, send_sem, recv_sem, {"seq": device}).wait_send()


def landed(ref, sem):
    pltpu.make_async_copy(ref, ref, sem).wait()


def each(start, stop, act):
    def step(i, carry):
        act(i)
        return carry

    lax.fori_loop(start, stop, step, 0)


def kernel(
    groups, norm,
    q_in, k_in, v_in, g_in,
    dq_out, dk_out, dv_out, qb_out, kvb_out,
    qs, gs, ks, vs, scores, dprobs, dqs, dkst, dvst, dqst, rk, rv, met,
    notes, notes_in, over_groups, groups_in, over_halves, halves_in,
    q_send, q_recv, k_send, k_recv, x_send, d_send, d_recv, m_send, m_recv, dq_send, dq_recv,
    n_send, n_recv, g_send, g_recv, h_send, h_recv,
):
    me = lax.axis_index("seq")
    group = lax.axis_index("dp")
    base = me // HALF * HALF
    index = me % HALF
    chunk = index // 2
    core = index % 2
    row = index // LINE
    column = chunk % 2
    beside = me + 2 - 4 * column
    opposite = (me + HALF) % (2 * HALF)

    barrier = pltpu.get_barrier_semaphore()

    def greet(device):
        pl.semaphore_signal(barrier, inc=1, device_id=device, device_id_type=MESH)

    each(1, HALF, lambda i: greet({"seq": base + (index + i) % HALF}))
    each(1, groups, lambda i: greet({"dp": (group + i) % groups}))
    greet({"seq": opposite})
    pl.semaphore_wait(barrier, HALF - 1 + groups - 1 + 1)

    def spread(act):
        for slot in range(SLOTS):
            for part in range(2):
                rows_in, rows_at = ((q_in, qs), (g_in, gs))[part]
                keys_in, keys_at = ((k_in, ks), (v_in, vs))[part]
                for to in range(2):
                    head = 2 * to + slot
                    act(
                        rows_in.at[:, pl.ds(head * COLS, COLS)],
                        rows_at.at[slot, at(core * ROWS, ROWS)],
                        q_send.at[head, part],
                        q_recv.at[slot, part],
                        base + chunk * 2 + to,
                        me,
                    )

                def push(line, there, lane):
                    for to in range(2):
                        head = 2 * to + slot
                        act(
                            keys_in.at[:, pl.ds(head * HEAD_SIZE, HEAD_SIZE)],
                            keys_at.at[slot, at(index * ROWS, ROWS)],
                            k_send.at[lane, head, part],
                            k_recv.at[slot, chunk, part],
                            base + (line * 2 + there) * 2 + to,
                            me,
                        )

                each(0, LINE - row, lambda i: push(LINE - 1 - i, column, LINE - 1 - i))

                @pl.when(column == 0)
                def _():
                    push(row, 1, LINE)

    def across(slot, part, line, act):
        place = (ks, vs)[part]
        block = place.at[slot, at((2 * line + column) * BLOCK, BLOCK)]
        sem = k_recv.at[slot, 2 * line + column, part]
        act(block, sem, x_send.at[slot, part, line])

    def hand_on(block, sem, out_sem):
        landed(block, sem)
        remote(block, block, out_sem, sem, {"seq": beside}).start()

    def handed_on(block, sem, out_sem):
        remote(block, block, out_sem, sem, {"seq": beside}).wait_send()

    spread(send)
    each(0, row, lambda i: across(0, 0, row - 1 - i, hand_on))

    first = 2 * row
    key_ids = lax.broadcasted_iota(jnp.int32, (BLOCK, BLOCK), 0)
    query_ids = lax.broadcasted_iota(jnp.int32, (BLOCK, BLOCK), 1)
    cols = [pl.ds(j * HEAD_SIZE, HEAD_SIZE) for j in range(GROUP)]

    def back(act, slot, block, place_at):
        head = 2 * core + slot
        for part in range(2):
            stage, place = ((dkst, rk), (dvst, rv))[part]
            for to in range(2):
                act(
                    stage.at[slot, at(block * BLOCK + to * ROWS, ROWS)],
                    place.at[place_at, :, at(head * HEAD_SIZE, HEAD_SIZE)],
                    d_send.at[slot, block, to, part],
                    d_recv.at[place_at, part],
                    base + block * 2 + to,
                    me,
                )

    def back_own(act, slot):
        back(act, slot, chunk, row)

        @pl.when(column == 1)
        def _():
            back(act, slot, first, LINE)

    def back_across(act, slot, line):
        block = 2 * line + 1 - column
        for part in range(2):
            act(
                (dkst, dvst)[part].at[slot, at(block * BLOCK, BLOCK)],
                met.at[slot, part, line],
                m_send.at[slot, part, line],
                m_recv.at[slot, part, line],
                beside,
                me,
            )

    def settle(slot, line):
        rows = at((2 * line + column) * BLOCK, BLOCK)
        for part in range(2):
            stage = (dkst, dvst)[part]
            landed(met.at[slot, part, line], m_recv.at[slot, part, line])
            total = stage[slot, rows, :].astype(F32) + met[slot, part, line].astype(F32)
            stage[slot, rows, :] = total.astype(BF16)
        back(send, slot, 2 * line + column, row)

    def back_rows(act, slot):
        head = 2 * core + slot
        for to in range(2):
            act(
                dqst.at[slot, pl.ds(to * ROWS, ROWS)],
                dq_out.at[:, at(head * COLS, COLS)],
                dq_send.at[slot, to],
                dq_recv,
                base + chunk * 2 + to,
                me,
            )

    def job(slot, carry):
        def wait_block(block, part):
            place = (ks, vs)[part]
            landed(place.at[slot, at(block * BLOCK, BLOCK)], k_recv.at[slot, block, part])

        def walk(step, part, carry, next_slot, next_part):
            wait_block(chunk, part)
            carry = step(chunk, 1, carry, True)

            def partner(i, c):
                wait_block(first, part)
                return step(first, 1, c, False)

            carry = lax.fori_loop(0, column, partner, carry)

            def below(i, c):
                line = row - 1 - i
                wait_block(2 * line + 1 - column, part)
                c = step(2 * line, 2, c, False)

                @pl.when(slot == 0)
                def _():
                    across(next_slot, next_part, line, hand_on)

                return c

            return lax.fori_loop(0, row, below, carry)

        def pass_scores(block, size, peaks, diagonal):
            rows = pl.ds(pl.multiple_of(block * BLOCK, BLOCK), size * BLOCK)
            key_block = ks[slot, rows, :]
            out = []
            for j in range(GROUP):
                s = dot(key_block, qs[slot, :, cols[j]], NT)
                if diagonal:
                    s = jnp.where(key_ids <= query_ids, s, -jnp.inf)
                scores[j, rows, :] = s
                out.append(jnp.maximum(peaks[j], fold(s, jnp.max)))
            return tuple(out)

        landed(qs.at[slot], q_recv.at[slot, 0])
        peaks = tuple(jnp.full((8, BLOCK), -jnp.inf, F32) for _ in range(GROUP))
        peaks = walk(pass_scores, 0, peaks, 0, 1)
        peaks = [jnp.max(x, axis=0, keepdims=True) * SCALE2 for x in peaks]

        def pass_probs(block, size, sums, diagonal):
            rows = pl.ds(pl.multiple_of(block * BLOCK, BLOCK), size * BLOCK)
            value_block = vs[slot, rows, :]
            out = []
            for j in range(GROUP):
                p = jnp.exp2(scores[j, rows, :] * SCALE2 - peaks[j])
                dp = dot(value_block, gs[slot, :, cols[j]], NT)
                scores[j, rows, :] = p
                dprobs[j, rows, :] = dp
                out.append((sums[j][0] + fold(p, jnp.sum), sums[j][1] + fold(p * dp, jnp.sum)))
            return tuple(out)

        landed(gs.at[slot], q_recv.at[slot, 1])
        zero = jnp.zeros((8, BLOCK), F32)
        sums = tuple((zero, zero) for _ in range(GROUP))
        sums = walk(pass_probs, 1, sums, 1, 0)
        inverse = [1.0 / jnp.sum(x[0], axis=0, keepdims=True) for x in sums]
        delta = [jnp.sum(x[1], axis=0, keepdims=True) * r for x, r in zip(sums, inverse)]

        dqs[...] = jnp.zeros_like(dqs)

        def pass_grads(block, size, bias):
            rows = pl.ds(pl.multiple_of(block * BLOCK, BLOCK), size * BLOCK)
            key_columns = ks[slot, rows, :].T
            dv = jnp.zeros((size * BLOCK, HEAD_SIZE), F32)
            dk = jnp.zeros((size * BLOCK, HEAD_SIZE), F32)
            for j in range(GROUP):
                p = scores[j, rows, :] * inverse[j]
                ds = (p * (dprobs[j, rows, :] - delta[j])).astype(BF16)
                dv = dv + dot(p.astype(BF16), gs[slot, :, cols[j]], NN)
                dk = dk + dot(ds, qs[slot, :, cols[j]], NN)
                dqs[j] += dot(key_columns, ds, NN)
            dk = dk * SCALE
            dkst[slot, rows, :] = dk.astype(BF16)
            dvst[slot, rows, :] = dv.astype(BF16)
            return bias[0] + fold(dk, jnp.sum), bias[1] + fold(dv, jnp.sum)

        def grads_below(line, bias):
            bias = pass_grads(2 * line, 2, bias)

            back_across(send, slot, line)

            @pl.when(line > 0)
            def _():
                @pl.when(slot * (line - 1) == 0)
                def _():
                    settle(slot, line - 1)

            @pl.when(slot == 0)
            def _():
                across(1, 1, line, hand_on)

            return bias

        zero = jnp.zeros((8, HEAD_SIZE), F32)
        bias = lax.fori_loop(0, row, grads_below, (zero, zero))
        bias = lax.fori_loop(first, chunk + 1, lambda b, c: pass_grads(b, 1, c), bias)

        @pl.when(slot == 0)
        def _():
            back_own(send, slot)

            @pl.when(row > 0)
            def _():
                settle(slot, row - 1)

        for part in range(2):
            notes[0, pl.ds(1 + 2 * slot + part, 1), :] = jnp.sum(bias[part], axis=0, keepdims=True)
        for j in range(GROUP):
            x = dqs[j] * SCALE
            x = x.T
            dqst[slot, :, cols[j]] = x.astype(BF16)
            notes[slot * GROUP + j, pl.ds(0, 1), :] = jnp.sum(
                fold(x, jnp.sum), axis=0, keepdims=True
            )
        return carry

    notes[...] = jnp.zeros_like(notes)
    lax.fori_loop(0, SLOTS, job, 0)

    for i in range(1, HALF):
        notes[i, pl.ds(1, 4), :] = notes[0, pl.ds(1, 4), :]

    def tell(i, act):
        act(notes.at[i], notes_in.at[index], n_send.at[i], n_recv, base + i, me)

    each(0, HALF, lambda i: tell(i, send))
    back_own(send, 1)
    each(row // 2, row, lambda line: settle(1, line))
    for slot in range(SLOTS):
        back_rows(send, slot)

    landed(notes_in, n_recv)
    sums = [notes_in[0], notes_in[1]]
    for i in range(2, HALF):
        sums[i % 2] = sums[i % 2] + notes_in[i]
    for i in range(2):
        over_groups[i] = sums[i]

    def to_group(i):
        return remote(
            over_groups, groups_in.at[i - 1], g_send.at[i - 1], g_recv, {"dp": (group + i) % groups}
        )

    each(1, groups, lambda i: to_group(i).start())
    landed(groups_in, g_recv)
    over_halves[...] = over_groups[...] + jnp.sum(groups_in[...], axis=0)
    to_half = remote(over_halves, halves_in, h_send, h_recv, {"seq": opposite})
    to_half.start()
    to_half.wait_recv()
    sums = (over_halves[...] + halves_in[...]) * norm
    qb_out[...] = jnp.where(base == 0, sums[0, 0:1], sums[1, 0:1])
    for head in range(KEYVALUE_HEADS):
        for part in range(2):
            at_row = 1 + 2 * (head % 2) + part
            kvb_out[pl.ds(part, 1), pl.ds(head * HEAD_SIZE, HEAD_SIZE)] = sums[
                head // 2, at_row : at_row + 1
            ]

    for part in range(2):
        place, out = ((rk, dk_out), (rv, dv_out))[part]

        def gather(source, so_far):
            landed(place.at[source], d_recv.at[source, part])
            return so_far + place[source].astype(F32)

        total = jnp.zeros((ROWS, KEYVALUE_HEADS * HEAD_SIZE), F32)
        out[...] = lax.fori_loop(row, LINE + 1 - column, gather, total).astype(BF16)

    landed(dq_out, dq_recv)

    spread(sent)
    for slot in range(SLOTS):
        for part in range(2):
            each(0, row, lambda line: across(slot, part, line, handed_on))
        back_own(sent, slot)
        each(0, row, lambda line: back(sent, slot, 2 * line + column, row))
        each(0, row, lambda line: back_across(sent, slot, line))
        back_rows(sent, slot)
    each(0, HALF, lambda i: tell(i, sent))
    each(1, groups, lambda i: to_group(i).wait_send())
    to_half.wait_send()


def local(query_input, key_input, value_input, output_gradient):
    groups = lax.axis_size("dp")
    norm = 1.0 / math.sqrt(ROWS * 2 * HALF * groups)
    vmem = pl.BlockSpec(memory_space=pltpu.VMEM)
    any_space = pl.BlockSpec(memory_space=pl.ANY)
    dma = pltpu.SemaphoreType.DMA
    kv_cols = KEYVALUE_HEADS * HEAD_SIZE
    return tuple(
        pl.pallas_call(
            functools.partial(kernel, groups, norm),
            out_shape=[
                jax.ShapeDtypeStruct((ROWS, QUERY_HEADS * HEAD_SIZE), BF16),
                jax.ShapeDtypeStruct((ROWS, kv_cols), BF16),
                jax.ShapeDtypeStruct((ROWS, kv_cols), BF16),
                jax.ShapeDtypeStruct((1, HEAD_SIZE), F32),
                jax.ShapeDtypeStruct((2, kv_cols), F32),
            ],
            in_specs=[any_space] * 4,
            out_specs=[any_space, vmem, vmem, vmem, vmem],
            scratch_shapes=[
                pltpu.VMEM((SLOTS, BLOCK, COLS), BF16),
                pltpu.VMEM((SLOTS, BLOCK, COLS), BF16),
                pltpu.VMEM((SLOTS, SPAN, HEAD_SIZE), BF16),
                pltpu.VMEM((SLOTS, SPAN, HEAD_SIZE), BF16),
                pltpu.VMEM((GROUP, SPAN, BLOCK), F32),
                pltpu.VMEM((GROUP, SPAN, BLOCK), F32),
                pltpu.VMEM((GROUP, HEAD_SIZE, BLOCK), F32),
                pltpu.VMEM((SLOTS, SPAN, HEAD_SIZE), BF16),
                pltpu.VMEM((SLOTS, SPAN, HEAD_SIZE), BF16),
                pltpu.VMEM((SLOTS, BLOCK, COLS), BF16),
                pltpu.VMEM((LINE + 1, ROWS, kv_cols), BF16),
                pltpu.VMEM((LINE + 1, ROWS, kv_cols), BF16),
                pltpu.VMEM((SLOTS, 2, LINE - 1, BLOCK, HEAD_SIZE), BF16),
                pltpu.VMEM((HALF, 8, HEAD_SIZE), F32),
                pltpu.VMEM((HALF, 8, HEAD_SIZE), F32),
                pltpu.VMEM((2, 8, HEAD_SIZE), F32),
                pltpu.VMEM((groups - 1, 2, 8, HEAD_SIZE), F32),
                pltpu.VMEM((2, 8, HEAD_SIZE), F32),
                pltpu.VMEM((2, 8, HEAD_SIZE), F32),
                dma((KEYVALUE_HEADS, 2)),
                dma((SLOTS, 2)),
                dma((LINE + 1, KEYVALUE_HEADS, 2)),
                dma((SLOTS, CHUNKS, 2)),
                dma((SLOTS, 2, LINE)),
                dma((SLOTS, CHUNKS, 2, 2)),
                dma((LINE + 1, 2)),
                dma((SLOTS, 2, LINE - 1)),
                dma((SLOTS, 2, LINE - 1)),
                dma((SLOTS, 2)),
                dma,
                dma((HALF,)),
                dma,
                dma((groups - 1,)),
                dma,
                dma,
                dma,
            ],
            compiler_params=pltpu.CompilerParams(
                collective_id=0, has_side_effects=True, vmem_limit_bytes=60 * 2**20
            ),
            name="attention_grads",
        )(query_input, key_input, value_input, output_gradient)
    )


def solution(mesh):
    rows = P(("dp", "seq"), None)
    return jax.shard_map(
        local,
        mesh=mesh,
        in_specs=(rows,) * 4,
        out_specs=(rows, rows, rows, P("seq", None), P()),
        check_vma=False,
    )
```

```python
import functools
import math

import jax
import jax.numpy as jnp
from jax import lax
from jax.experimental import pallas as pl
from jax.experimental.pallas import tpu as pltpu
from jax.sharding import PartitionSpec as P

QUERY_HEADS = 32
KEYVALUE_HEADS = 4
HEAD_SIZE = 128
GROUP = QUERY_HEADS // KEYVALUE_HEADS
ROWS = 128
BLOCK = 256
CHUNKS = 8
SPAN = BLOCK * CHUNKS
HALF = 16
MEMBERS = 2 * HALF
SLOTS = 2
NOTE = 5
LINE = 4
COLS = GROUP * HEAD_SIZE
SCALE = 1.0 / math.sqrt(HEAD_SIZE)
SCALE2 = SCALE * math.log2(math.e)

F32 = jnp.float32
BF16 = jnp.bfloat16
MESH = pl.DeviceIdType.MESH
NT = (((1,), (1,)), ((), ()))
NN = (((1,), (0,)), ((), ()))
TN = (((0,), (0,)), ((), ()))


def dot(a, b, dims):
    return lax.dot_general(a, b, dims, preferred_element_type=F32)


def fold(x, op):
    return op(x.reshape(x.shape[0] // 8, 8, x.shape[1]), axis=0)


def at(start, size):
    return pl.ds(pl.multiple_of(start, size), size)


def remote(src, dst, send_sem, recv_sem, device):
    return pltpu.make_async_remote_copy(
        src, dst, send_sem, recv_sem, device_id=device, device_id_type=MESH
    )


def send(src, dst, send_sem, recv_sem, device, me):
    @pl.when(device != me)
    def _():
        remote(src, dst, send_sem, recv_sem, {"seq": device}).start()

    @pl.when(device == me)
    def _():
        pltpu.make_async_copy(src, dst, recv_sem).start()


def sent(src, dst, send_sem, recv_sem, device, me):
    @pl.when(device != me)
    def _():
        remote(src, dst, send_sem, recv_sem, {"seq": device}).wait_send()


def landed(ref, sem):
    pltpu.make_async_copy(ref, ref, sem).wait()


def each(start, stop, act):
    def step(i, carry):
        act(i)
        return carry

    lax.fori_loop(start, stop, step, 0)


def kernel(
    groups, norm,
    q_in, k_in, v_in, g_in,
    dq_out, dk_out, dv_out, qb_out, kvb_out,
    qs, gs, ks, vs, scores, dprobs, dqs, dkst, dvst, dqst, rk, rv, met,
    notes, notes_in, over_groups, groups_in,
    q_send, q_recv, k_send, k_recv, x_send, d_send, d_recv, m_send, m_recv, dq_send, dq_recv,
    n_send, n_recv, g_send, g_recv,
):
    me = lax.axis_index("seq")
    group = lax.axis_index("dp")
    base = me // HALF * HALF
    index = me % HALF
    chunk = index // 2
    core = index % 2
    row = index // LINE
    column = chunk % 2
    beside = me + 2 - 4 * column
    above = me + LINE - MEMBERS * (me // (MEMBERS - LINE))

    barrier = pltpu.get_barrier_semaphore()

    def greet(device):
        pl.semaphore_signal(barrier, inc=1, device_id=device, device_id_type=MESH)

    each(1, MEMBERS, lambda i: greet({"seq": (me + i) % MEMBERS}))
    each(1, groups, lambda i: greet({"dp": (group + i) % groups}))
    pl.semaphore_wait(barrier, MEMBERS - 1 + groups - 1)

    def spread(act):
        for slot in range(SLOTS):
            for part in range(2):
                rows_in, rows_at = ((q_in, qs), (g_in, gs))[part]
                keys_in, keys_at = ((k_in, ks), (v_in, vs))[part]
                for to in range(2):
                    head = 2 * to + slot
                    act(
                        rows_in.at[:, pl.ds(head * COLS, COLS)],
                        rows_at.at[slot, at(core * ROWS, ROWS)],
                        q_send.at[head, part],
                        q_recv.at[slot, part],
                        base + chunk * 2 + to,
                        me,
                    )

                def push(line, there, lane):
                    for to in range(2):
                        head = 2 * to + slot
                        act(
                            keys_in.at[:, pl.ds(head * HEAD_SIZE, HEAD_SIZE)],
                            keys_at.at[slot, at(index * ROWS, ROWS)],
                            k_send.at[lane, head, part],
                            k_recv.at[slot, chunk, part],
                            base + (line * 2 + there) * 2 + to,
                            me,
                        )

                push(row, column, 0)

                @pl.when(row < LINE - 1)
                def _():
                    push(row + 1, column, 1)

                @pl.when(column == 0)
                def _():
                    push(row, 1, 2)

    def pass_on(slot, part, line, act):
        block = (ks, vs)[part].at[slot, at((2 * line + column) * BLOCK, BLOCK)]
        sem = k_recv.at[slot, 2 * line + column, part]
        act(block, sem, x_send.at[slot, part, line])

    def hand_on(block, sem, out_sem):
        landed(block, sem)

        @pl.when(row < LINE - 1)
        def _():
            remote(block, block, out_sem.at[1], sem, {"seq": above}).start()

        remote(block, block, out_sem.at[0], sem, {"seq": beside}).start()

    def handed_on(block, sem, out_sem):
        @pl.when(row < LINE - 1)
        def _():
            remote(block, block, out_sem.at[1], sem, {"seq": above}).wait_send()

        remote(block, block, out_sem.at[0], sem, {"seq": beside}).wait_send()

    spread(send)
    each(0, row, lambda i: pass_on(0, 0, row - 1 - i, hand_on))

    first = 2 * row
    key_ids = lax.broadcasted_iota(jnp.int32, (BLOCK, BLOCK), 0)
    query_ids = lax.broadcasted_iota(jnp.int32, (BLOCK, BLOCK), 1)
    cols = [pl.ds(j * HEAD_SIZE, HEAD_SIZE) for j in range(GROUP)]

    def back(act, slot, block, place_at):
        head = 2 * core + slot
        for part in range(2):
            stage, place = ((dkst, rk), (dvst, rv))[part]
            for to in range(2):
                act(
                    stage.at[slot, at(block * BLOCK + to * ROWS, ROWS)],
                    place.at[place_at, :, at(head * HEAD_SIZE, HEAD_SIZE)],
                    d_send.at[slot, block, to, part],
                    d_recv.at[place_at, part],
                    base + block * 2 + to,
                    me,
                )

    def back_own(act, slot):
        back(act, slot, chunk, row)

        @pl.when(column == 1)
        def _():
            back(act, slot, first, LINE)

    def back_across(act, slot, line):
        block = 2 * line + 1 - column
        for part in range(2):
            act(
                (dkst, dvst)[part].at[slot, at(block * BLOCK, BLOCK)],
                met.at[slot, part, line],
                m_send.at[slot, part, line],
                m_recv.at[slot, part, line],
                beside,
                me,
            )

    def settle(slot, line):
        rows = at((2 * line + column) * BLOCK, BLOCK)
        for part in range(2):
            stage = (dkst, dvst)[part]
            landed(met.at[slot, part, line], m_recv.at[slot, part, line])
            total = stage[slot, rows, :].astype(F32) + met[slot, part, line].astype(F32)
            stage[slot, rows, :] = total.astype(BF16)
        back(send, slot, 2 * line + column, row)

    def back_rows(act, slot):
        head = 2 * core + slot
        for to in range(2):
            act(
                dqst.at[slot, pl.ds(to * ROWS, ROWS)],
                dq_out.at[:, at(head * COLS, COLS)],
                dq_send.at[slot, to],
                dq_recv,
                base + chunk * 2 + to,
                me,
            )

    def job(slot, carry):
        def wait_block(block, part):
            place = (ks, vs)[part]
            landed(place.at[slot, at(block * BLOCK, BLOCK)], k_recv.at[slot, block, part])

        def walk(step, part, carry, next_slot, next_part):
            wait_block(chunk, part)
            carry = step(chunk, 1, carry, True)

            def partner(i, c):
                wait_block(first, part)
                return step(first, 1, c, False)

            carry = lax.fori_loop(0, column, partner, carry)

            def below(i, c):
                line = row - 1 - i
                wait_block(2 * line + 1 - column, part)
                c = step(2 * line, 2, c, False)
                if part == 0:

                    @pl.when(slot == 1)
                    def _():
                        settle(0, line)

                @pl.when(slot == 0)
                def _():
                    pass_on(next_slot, next_part, line, hand_on)

                return c

            return lax.fori_loop(0, row, below, carry)

        def pass_scores(block, size, peaks, diagonal):
            rows = pl.ds(pl.multiple_of(block * BLOCK, BLOCK), size * BLOCK)
            key_block = ks[slot, rows, :]
            out = []
            for j in range(GROUP):
                s = dot(key_block, qs[slot, :, cols[j]], NT)
                if diagonal:
                    s = jnp.where(key_ids <= query_ids, s, -jnp.inf)
                scores[j, rows, :] = s
                out.append(jnp.maximum(peaks[j], fold(s, jnp.max)))
            return tuple(out)

        landed(qs.at[slot], q_recv.at[slot, 0])
        peaks = tuple(jnp.full((8, BLOCK), -jnp.inf, F32) for _ in range(GROUP))
        peaks = walk(pass_scores, 0, peaks, 0, 1)
        peaks = [jnp.max(x, axis=0, keepdims=True) * SCALE2 for x in peaks]

        def pass_probs(block, size, sums, diagonal):
            rows = pl.ds(pl.multiple_of(block * BLOCK, BLOCK), size * BLOCK)
            value_block = vs[slot, rows, :]
            out = []
            for j in range(GROUP):
                p = jnp.exp2(scores[j, rows, :] * SCALE2 - peaks[j])
                dp = dot(value_block, gs[slot, :, cols[j]], NT)
                scores[j, rows, :] = p
                dprobs[j, rows, :] = dp
                out.append((sums[j][0] + fold(p, jnp.sum), sums[j][1] + fold(p * dp, jnp.sum)))
            return tuple(out)

        landed(gs.at[slot], q_recv.at[slot, 1])
        zero = jnp.zeros((8, BLOCK), F32)
        sums = tuple((zero, zero) for _ in range(GROUP))
        sums = walk(pass_probs, 1, sums, 1, 0)
        inverse = [1.0 / jnp.sum(x[0], axis=0, keepdims=True) for x in sums]
        delta = [jnp.sum(x[1], axis=0, keepdims=True) * r for x, r in zip(sums, inverse)]

        dqs[...] = jnp.zeros_like(dqs)

        def pass_grads(block, size, bias):
            rows = pl.ds(pl.multiple_of(block * BLOCK, BLOCK), size * BLOCK)
            key_columns = ks[slot, rows, :].T
            dv = jnp.zeros((size * BLOCK, HEAD_SIZE), F32)
            dk = jnp.zeros((size * BLOCK, HEAD_SIZE), F32)
            for j in range(GROUP):
                p = scores[j, rows, :] * inverse[j]
                ds = (p * (dprobs[j, rows, :] - delta[j])).astype(BF16)
                dv = dv + dot(p.astype(BF16), gs[slot, :, cols[j]], NN)
                dk = dk + dot(ds, qs[slot, :, cols[j]], NN)
                dqs[j] += dot(key_columns, ds, NN)
            dk = dk * SCALE
            dkst[slot, rows, :] = dk.astype(BF16)
            dvst[slot, rows, :] = dv.astype(BF16)
            return bias[0] + fold(dk, jnp.sum), bias[1] + fold(dv, jnp.sum)

        def grads_below(line, bias):
            bias = pass_grads(2 * line, 2, bias)

            back_across(send, slot, line)

            @pl.when(slot * line > 1)
            def _():
                settle(1, line - 2)

            @pl.when(slot == 0)
            def _():
                pass_on(1, 1, line, hand_on)

            return bias

        zero = jnp.zeros((8, HEAD_SIZE), F32)
        bias = lax.fori_loop(0, row, grads_below, (zero, zero))
        bias = lax.fori_loop(first, chunk + 1, lambda b, c: pass_grads(b, 1, c), bias)

        @pl.when(slot == 0)
        def _():
            back_own(send, 0)

        for part in range(2):
            notes[0, 1 + 2 * slot + part] = jnp.sum(bias[part], axis=0, keepdims=True)
        for j in range(GROUP):
            x = dqs[j] * SCALE
            x = x.T
            dqst[slot, :, cols[j]] = x.astype(BF16)
            notes[slot * GROUP + j, 0] = jnp.sum(fold(x, jnp.sum), axis=0, keepdims=True)
        return carry

    notes[...] = jnp.zeros_like(notes)
    lax.fori_loop(0, SLOTS, job, 0)

    for i in range(1, HALF):
        for j in range(1, NOTE):
            notes[i, j] = notes[0, j]

    def tell(i, act):
        act(notes.at[i % HALF], notes_in.at[me], n_send.at[i], n_recv, i, me)

    each(0, MEMBERS, lambda i: tell(i, send))
    back_own(send, 1)
    each(row // 3, row, lambda line: settle(1, line))
    for slot in range(SLOTS):
        back_rows(send, slot)

    landed(notes_in, n_recv)
    sums = [notes_in[0], notes_in[1]]
    for i in range(2, MEMBERS):
        sums[i % 2] = sums[i % 2] + notes_in[i]
    over_groups[0] = jnp.where(base == 0, sums[0][0], sums[1][0])
    for i in range(2):
        for j in range(1, NOTE):
            over_groups[i * (NOTE - 1) + j] = sums[i][j]

    def to_group(i):
        return remote(
            over_groups, groups_in.at[i - 1], g_send.at[i - 1], g_recv, {"dp": (group + i) % groups}
        )

    each(1, groups, lambda i: to_group(i).start())
    landed(groups_in, g_recv)
    sums = (over_groups[...] + jnp.sum(groups_in[...], axis=0)) * norm
    qb_out[...] = sums[0]
    for head in range(KEYVALUE_HEADS):
        for part in range(2):
            kvb_out[pl.ds(part, 1), pl.ds(head * HEAD_SIZE, HEAD_SIZE)] = sums[1 + 2 * head + part]

    for part in range(2):
        place, out = ((rk, dk_out), (rv, dv_out))[part]

        def gather(source, so_far):
            landed(place.at[source], d_recv.at[source, part])
            return so_far + place[source].astype(F32)

        total = jnp.zeros((ROWS, KEYVALUE_HEADS * HEAD_SIZE), F32)
        out[...] = lax.fori_loop(row, LINE + 1 - column, gather, total).astype(BF16)

    landed(dq_out, dq_recv)

    spread(sent)
    for slot in range(SLOTS):
        for part in range(2):
            each(0, row, lambda line: pass_on(slot, part, line, handed_on))
        back_own(sent, slot)
        each(0, row, lambda line: back(sent, slot, 2 * line + column, row))
        each(0, row, lambda line: back_across(sent, slot, line))
        back_rows(sent, slot)
    each(0, MEMBERS, lambda i: tell(i, sent))
    each(1, groups, lambda i: to_group(i).wait_send())


def hand_out(*refs):
    *refs, sems = refs
    count = len(refs) // 2
    copies = [pltpu.make_async_copy(refs[i], refs[count + i], sems.at[i]) for i in range(count)]
    for copy in copies:
        copy.start()
    for copy in copies:
        copy.wait()


def local(query_input, key_input, value_input, output_gradient):
    groups = lax.axis_size("dp")
    norm = 1.0 / math.sqrt(ROWS * MEMBERS * groups)
    vmem = pl.BlockSpec(memory_space=pltpu.VMEM)
    any_space = pl.BlockSpec(memory_space=pl.ANY)
    dma = pltpu.SemaphoreType.DMA
    kv_cols = KEYVALUE_HEADS * HEAD_SIZE
    results = tuple(
        pl.pallas_call(
            functools.partial(kernel, groups, norm),
            out_shape=[
                jax.ShapeDtypeStruct((ROWS, QUERY_HEADS * HEAD_SIZE), BF16),
                jax.ShapeDtypeStruct((ROWS, kv_cols), BF16),
                jax.ShapeDtypeStruct((ROWS, kv_cols), BF16),
                jax.ShapeDtypeStruct((1, HEAD_SIZE), F32),
                jax.ShapeDtypeStruct((2, kv_cols), F32),
            ],
            in_specs=[any_space] * 4,
            out_specs=[any_space, vmem, vmem, vmem, vmem],
            scratch_shapes=[
                pltpu.VMEM((SLOTS, BLOCK, COLS), BF16),
                pltpu.VMEM((SLOTS, BLOCK, COLS), BF16),
                pltpu.VMEM((SLOTS, SPAN, HEAD_SIZE), BF16),
                pltpu.VMEM((SLOTS, SPAN, HEAD_SIZE), BF16),
                pltpu.VMEM((GROUP, SPAN, BLOCK), F32),
                pltpu.VMEM((GROUP, SPAN, BLOCK), F32),
                pltpu.VMEM((GROUP, HEAD_SIZE, BLOCK), F32),
                pltpu.VMEM((SLOTS, SPAN, HEAD_SIZE), BF16),
                pltpu.VMEM((SLOTS, SPAN, HEAD_SIZE), BF16),
                pltpu.VMEM((SLOTS, BLOCK, COLS), BF16),
                pltpu.VMEM((LINE + 1, ROWS, kv_cols), BF16),
                pltpu.VMEM((LINE + 1, ROWS, kv_cols), BF16),
                pltpu.VMEM((SLOTS, 2, LINE - 1, BLOCK, HEAD_SIZE), BF16),
                pltpu.VMEM((HALF, NOTE, 1, HEAD_SIZE), F32),
                pltpu.VMEM((MEMBERS, NOTE, 1, HEAD_SIZE), F32),
                pltpu.VMEM((2 * NOTE - 1, 1, HEAD_SIZE), F32),
                pltpu.VMEM((groups - 1, 2 * NOTE - 1, 1, HEAD_SIZE), F32),
                dma((KEYVALUE_HEADS, 2)),
                dma((SLOTS, 2)),
                dma((3, KEYVALUE_HEADS, 2)),
                dma((SLOTS, CHUNKS, 2)),
                dma((SLOTS, 2, LINE - 1, 2)),
                dma((SLOTS, CHUNKS, 2, 2)),
                dma((LINE + 1, 2)),
                dma((SLOTS, 2, LINE - 1)),
                dma((SLOTS, 2, LINE - 1)),
                dma((SLOTS, 2)),
                dma,
                dma((MEMBERS,)),
                dma,
                dma((groups - 1,)),
                dma,
            ],
            compiler_params=pltpu.CompilerParams(
                collective_id=0, has_side_effects=True, vmem_limit_bytes=60 * 2**20
            ),
            name="attention_grads",
        )(query_input, key_input, value_input, output_gradient)
    )
    return tuple(
        pl.pallas_call(
            hand_out,
            out_shape=[jax.ShapeDtypeStruct(x.shape, x.dtype) for x in results],
            in_specs=[vmem] * len(results),
            out_specs=[any_space] * len(results),
            scratch_shapes=[dma((len(results),))],
            name="hand_out",
        )(*results)
    )


def solution(mesh):
    rows = P(("dp", "seq"), None)
    return jax.shard_map(
        local,
        mesh=mesh,
        in_specs=(rows,) * 4,
        out_specs=(rows, rows, rows, P("seq", None), P()),
        check_vma=False,
    )
```

```python
import functools
import math

import jax
import jax.numpy as jnp
from jax import lax
from jax.experimental import pallas as pl
from jax.experimental.pallas import tpu as pltpu
from jax.sharding import PartitionSpec as P

QUERY_HEADS = 32
KEYVALUE_HEADS = 4
HEAD_SIZE = 128
GROUP = QUERY_HEADS // KEYVALUE_HEADS
ROWS = 128
BLOCK = 256
CHUNKS = 8
SPAN = BLOCK * CHUNKS
HALF = 16
MEMBERS = 2 * HALF
SLOTS = 2
NOTE = 5
LINE = 4
COLS = GROUP * HEAD_SIZE
SCALE = 1.0 / math.sqrt(HEAD_SIZE)
SCALE2 = SCALE * math.log2(math.e)

F32 = jnp.float32
BF16 = jnp.bfloat16
MESH = pl.DeviceIdType.MESH
NT = (((1,), (1,)), ((), ()))
NN = (((1,), (0,)), ((), ()))
TN = (((0,), (0,)), ((), ()))


def dot(a, b, dims):
    return lax.dot_general(a, b, dims, preferred_element_type=F32)


def fold(x, op):
    return op(x.reshape(x.shape[0] // 8, 8, x.shape[1]), axis=0)


def at(start, size):
    return pl.ds(pl.multiple_of(start, size), size)


def remote(src, dst, send_sem, recv_sem, device):
    return pltpu.make_async_remote_copy(
        src, dst, send_sem, recv_sem, device_id=device, device_id_type=MESH
    )


def send(src, dst, send_sem, recv_sem, device, me):
    @pl.when(device != me)
    def _():
        remote(src, dst, send_sem, recv_sem, {"seq": device}).start()

    @pl.when(device == me)
    def _():
        pltpu.make_async_copy(src, dst, recv_sem).start()


def sent(src, dst, send_sem, recv_sem, device, me):
    @pl.when(device != me)
    def _():
        remote(src, dst, send_sem, recv_sem, {"seq": device}).wait_send()


def landed(ref, sem):
    pltpu.make_async_copy(ref, ref, sem).wait()


def each(start, stop, act):
    def step(i, carry):
        act(i)
        return carry

    lax.fori_loop(start, stop, step, 0)


def kernel(
    groups, norm,
    q_in, k_in, v_in, g_in,
    dq_out, dk_out, dv_out, qb_out, kvb_out,
    qs, gs, ks, vs, scores, dprobs, dqs, dkst, dvst, dqst, rk, rv, met,
    notes, notes_in, over_groups, groups_in,
    q_send, q_recv, k_send, k_recv, x_send, d_send, d_recv, m_send, m_recv, dq_send, dq_recv,
    n_send, n_recv, g_send, g_recv,
):
    me = lax.axis_index("seq")
    group = lax.axis_index("dp")
    base = me // HALF * HALF
    index = me % HALF
    chunk = index // 2
    core = index % 2
    row = index // LINE
    column = chunk % 2
    beside = me + 2 - 4 * column
    above = me + LINE - MEMBERS * (me // (MEMBERS - LINE))

    barrier = pltpu.get_barrier_semaphore()

    def greet(device):
        pl.semaphore_signal(barrier, inc=1, device_id=device, device_id_type=MESH)

    each(1, MEMBERS, lambda i: greet({"seq": (me + i) % MEMBERS}))
    each(1, groups, lambda i: greet({"dp": (group + i) % groups}))
    pl.semaphore_wait(barrier, MEMBERS - 1 + groups - 1)

    def spread(act):
        for slot in range(SLOTS):
            for part in range(2):
                rows_in, rows_at = ((q_in, qs), (g_in, gs))[part]
                keys_in, keys_at = ((k_in, ks), (v_in, vs))[part]
                def push(line, there, lane):
                    for to in range(2):
                        head = 2 * to + slot
                        act(
                            keys_in.at[:, pl.ds(head * HEAD_SIZE, HEAD_SIZE)],
                            keys_at.at[slot, at(index * ROWS, ROWS)],
                            k_send.at[lane, head, part],
                            k_recv.at[slot, chunk, part],
                            base + (line * 2 + there) * 2 + to,
                            me,
                        )

                @pl.when(row < LINE - 1)
                def _():
                    push(row + 1, column, 1)

                push(row, column, 0)

                @pl.when(column == 0)
                def _():
                    push(row, 1, 2)

                for to in range(2):
                    head = 2 * to + slot
                    act(
                        rows_in.at[:, pl.ds(head * COLS, COLS)],
                        rows_at.at[slot, at(core * ROWS, ROWS)],
                        q_send.at[head, part],
                        q_recv.at[slot, part],
                        base + chunk * 2 + to,
                        me,
                    )

    def pass_on(slot, part, line, act):
        block = (ks, vs)[part].at[slot, at((2 * line + column) * BLOCK, BLOCK)]
        sem = k_recv.at[slot, 2 * line + column, part]
        act(block, sem, x_send.at[slot, part, line])

    def hand_on(block, sem, out_sem):
        landed(block, sem)

        @pl.when(row < LINE - 1)
        def _():
            remote(block, block, out_sem.at[1], sem, {"seq": above}).start()

        remote(block, block, out_sem.at[0], sem, {"seq": beside}).start()

    def handed_on(block, sem, out_sem):
        @pl.when(row < LINE - 1)
        def _():
            remote(block, block, out_sem.at[1], sem, {"seq": above}).wait_send()

        remote(block, block, out_sem.at[0], sem, {"seq": beside}).wait_send()

    spread(send)
    top = row // (LINE - 1)

    def first_keys(count):
        each(0, count, lambda i: pass_on(0, 0, row - 1 - i, hand_on))

    first_keys(row * (1 - top))

    first = 2 * row
    key_ids = lax.broadcasted_iota(jnp.int32, (BLOCK, BLOCK), 0)
    query_ids = lax.broadcasted_iota(jnp.int32, (BLOCK, BLOCK), 1)
    cols = [pl.ds(j * HEAD_SIZE, HEAD_SIZE) for j in range(GROUP)]

    def back(act, slot, block, place_at):
        head = 2 * core + slot
        for part in range(2):
            stage, place = ((dkst, rk), (dvst, rv))[part]
            for to in range(2):
                act(
                    stage.at[slot, at(block * BLOCK + to * ROWS, ROWS)],
                    place.at[place_at, :, at(head * HEAD_SIZE, HEAD_SIZE)],
                    d_send.at[slot, block, to, part],
                    d_recv.at[place_at, part],
                    base + block * 2 + to,
                    me,
                )

    def back_own(act, slot):
        back(act, slot, chunk, row)

        @pl.when(column == 1)
        def _():
            back(act, slot, first, LINE)

    def back_across(act, slot, line):
        block = 2 * line + 1 - column
        for part in range(2):
            act(
                (dkst, dvst)[part].at[slot, at(block * BLOCK, BLOCK)],
                met.at[slot, part, line],
                m_send.at[slot, part, line],
                m_recv.at[slot, part, line],
                beside,
                me,
            )

    def settle(slot, line):
        rows = at((2 * line + column) * BLOCK, BLOCK)
        for part in range(2):
            stage = (dkst, dvst)[part]
            landed(met.at[slot, part, line], m_recv.at[slot, part, line])
            total = stage[slot, rows, :].astype(F32) + met[slot, part, line].astype(F32)
            stage[slot, rows, :] = total.astype(BF16)
        back(send, slot, 2 * line + column, row)

    def back_rows(act, slot):
        head = 2 * core + slot
        for to in range(2):
            act(
                dqst.at[slot, pl.ds(to * ROWS, ROWS)],
                dq_out.at[:, at(head * COLS, COLS)],
                dq_send.at[slot, to],
                dq_recv,
                base + chunk * 2 + to,
                me,
            )

    def job(slot, carry):
        def wait_block(block, part):
            place = (ks, vs)[part]
            landed(place.at[slot, at(block * BLOCK, BLOCK)], k_recv.at[slot, block, part])

        def walk(step, part, carry, next_slot, next_part):
            wait_block(chunk, part)

            def both(i, c):
                wait_block(first, part)
                return step(first, 2, c, True)

            carry = lax.fori_loop(0, column, both, carry)
            carry = lax.fori_loop(0, 1 - column, lambda i, c: step(first, 1, c, True), carry)
            if part == 0:

                @pl.when(slot == 0)
                def _():
                    first_keys(row * top)

            def below(i, c):
                line = row - 1 - i
                wait_block(2 * line + 1 - column, part)
                c = step(2 * line, 2, c, False)
                if part == 0:

                    @pl.when(slot == 1)
                    def _():
                        settle(0, line)

                @pl.when(slot == 0)
                def _():
                    pass_on(next_slot, next_part, line, hand_on)

                return c

            return lax.fori_loop(0, row, below, carry)

        def pass_scores(block, size, peaks, diagonal):
            rows = pl.ds(pl.multiple_of(block * BLOCK, BLOCK), size * BLOCK)
            key_block = ks[slot, rows, :]
            out = []
            for j in range(GROUP):
                s = dot(key_block, qs[slot, :, cols[j]], NT)
                if diagonal:
                    edge = (size - 1) * BLOCK
                    tail = jnp.where(key_ids <= query_ids, s[edge:], -jnp.inf)
                    s = jnp.concatenate([s[:edge], tail], axis=0) if edge else tail
                scores[j, rows, :] = s
                out.append(jnp.maximum(peaks[j], fold(s, jnp.max)))
            return tuple(out)

        landed(qs.at[slot], q_recv.at[slot, 0])
        peaks = tuple(jnp.full((8, BLOCK), -jnp.inf, F32) for _ in range(GROUP))
        peaks = walk(pass_scores, 0, peaks, 0, 1)
        peaks = [jnp.max(x, axis=0, keepdims=True) * SCALE2 for x in peaks]

        def pass_probs(block, size, sums, diagonal):
            rows = pl.ds(pl.multiple_of(block * BLOCK, BLOCK), size * BLOCK)
            value_block = vs[slot, rows, :]
            out = []
            for j in range(GROUP):
                p = jnp.exp2(scores[j, rows, :] * SCALE2 - peaks[j])
                dp = dot(value_block, gs[slot, :, cols[j]], NT)
                scores[j, rows, :] = p
                dprobs[j, rows, :] = dp
                out.append((sums[j][0] + fold(p, jnp.sum), sums[j][1] + fold(p * dp, jnp.sum)))
            return tuple(out)

        landed(gs.at[slot], q_recv.at[slot, 1])
        zero = jnp.zeros((8, BLOCK), F32)
        sums = tuple((zero, zero) for _ in range(GROUP))
        sums = walk(pass_probs, 1, sums, 1, 0)
        inverse = [1.0 / jnp.sum(x[0], axis=0, keepdims=True) for x in sums]
        delta = [jnp.sum(x[1], axis=0, keepdims=True) * r for x, r in zip(sums, inverse)]

        dqs[...] = jnp.zeros_like(dqs)

        def pass_grads(block, size, bias):
            rows = pl.ds(pl.multiple_of(block * BLOCK, BLOCK), size * BLOCK)
            key_columns = ks[slot, rows, :].T
            dv = jnp.zeros((size * BLOCK, HEAD_SIZE), F32)
            dk = jnp.zeros((size * BLOCK, HEAD_SIZE), F32)
            for j in range(GROUP):
                p = scores[j, rows, :] * inverse[j]
                ds = (p * (dprobs[j, rows, :] - delta[j])).astype(BF16)
                dv = dv + dot(p.astype(BF16), gs[slot, :, cols[j]], NN)
                dk = dk + dot(ds, qs[slot, :, cols[j]], NN)
                dqs[j] += dot(key_columns, ds, NN)
            dk = dk * SCALE
            dkst[slot, rows, :] = dk.astype(BF16)
            dvst[slot, rows, :] = dv.astype(BF16)
            return bias[0] + fold(dk, jnp.sum), bias[1] + fold(dv, jnp.sum)

        def grads_below(line, bias):
            bias = pass_grads(2 * line, 2, bias)

            back_across(send, slot, line)

            @pl.when(slot * line > 1)
            def _():
                settle(1, line - 2)

            @pl.when(slot == 0)
            def _():
                pass_on(1, 1, line, hand_on)

            return bias

        zero = jnp.zeros((8, HEAD_SIZE), F32)
        bias = lax.fori_loop(0, row, grads_below, (zero, zero))
        bias = lax.fori_loop(0, column, lambda i, c: pass_grads(first, 2, c), bias)
        bias = lax.fori_loop(0, 1 - column, lambda i, c: pass_grads(first, 1, c), bias)

        @pl.when(slot == 0)
        def _():
            back_own(send, 0)

        for part in range(2):
            notes[0, 1 + 2 * slot + part] = jnp.sum(bias[part], axis=0, keepdims=True)
        for j in range(GROUP):
            x = dqs[j] * SCALE
            x = x.T
            dqst[slot, :, cols[j]] = x.astype(BF16)
            notes[slot * GROUP + j, 0] = jnp.sum(fold(x, jnp.sum), axis=0, keepdims=True)

        @pl.when(slot == 0)
        def _():
            back_rows(send, 0)

        return carry

    notes[...] = jnp.zeros_like(notes)
    lax.fori_loop(0, SLOTS, job, 0)

    for i in range(1, HALF):
        for j in range(1, NOTE):
            notes[i, j] = notes[0, j]

    def tell(i, act):
        act(notes.at[i % HALF], notes_in.at[me], n_send.at[i], n_recv, i, me)

    each(0, MEMBERS, lambda i: tell(i, send))
    back_own(send, 1)
    each(row // 3, row, lambda line: settle(1, line))
    back_rows(send, 1)

    def back_all(slot):
        back_own(sent, slot)
        each(0, row, lambda line: back(sent, slot, 2 * line + column, row))
        each(0, row, lambda line: back_across(sent, slot, line))
        back_rows(sent, slot)

    spread(sent)
    for slot in range(SLOTS):
        for part in range(2):
            each(0, row, lambda line: pass_on(slot, part, line, handed_on))
    back_all(0)

    landed(notes_in, n_recv)
    sums = [notes_in[0], notes_in[1]]
    for i in range(2, MEMBERS):
        sums[i % 2] = sums[i % 2] + notes_in[i]
    over_groups[0] = jnp.where(base == 0, sums[0][0], sums[1][0])
    for i in range(2):
        for j in range(1, NOTE):
            over_groups[i * (NOTE - 1) + j] = sums[i][j]

    def to_group(i):
        return remote(
            over_groups, groups_in.at[i - 1], g_send.at[i - 1], g_recv, {"dp": (group + i) % groups}
        )

    each(1, groups, lambda i: to_group(i).start())
    each(0, MEMBERS, lambda i: tell(i, sent))
    landed(groups_in, g_recv)
    sums = (over_groups[...] + jnp.sum(groups_in[...], axis=0)) * norm
    qb_out[...] = sums[0]
    for head in range(KEYVALUE_HEADS):
        for part in range(2):
            kvb_out[pl.ds(part, 1), pl.ds(head * HEAD_SIZE, HEAD_SIZE)] = sums[1 + 2 * head + part]

    for part in range(2):
        place, out = ((rk, dk_out), (rv, dv_out))[part]

        def gather(source, so_far):
            landed(place.at[source], d_recv.at[source, part])
            return so_far + place[source].astype(F32)

        total = jnp.zeros((ROWS, KEYVALUE_HEADS * HEAD_SIZE), F32)
        out[...] = lax.fori_loop(row, LINE + 1 - column, gather, total).astype(BF16)

    landed(dq_out, dq_recv)

    back_all(1)
    each(1, groups, lambda i: to_group(i).wait_send())


def hand_out(*refs):
    *refs, sems = refs
    count = len(refs) // 2
    copies = [pltpu.make_async_copy(refs[i], refs[count + i], sems.at[i]) for i in range(count)]
    for copy in copies:
        copy.start()
    for copy in copies:
        copy.wait()


def local(query_input, key_input, value_input, output_gradient):
    groups = lax.axis_size("dp")
    norm = 1.0 / math.sqrt(ROWS * MEMBERS * groups)
    vmem = pl.BlockSpec(memory_space=pltpu.VMEM)
    any_space = pl.BlockSpec(memory_space=pl.ANY)
    dma = pltpu.SemaphoreType.DMA
    kv_cols = KEYVALUE_HEADS * HEAD_SIZE
    results = tuple(
        pl.pallas_call(
            functools.partial(kernel, groups, norm),
            out_shape=[
                jax.ShapeDtypeStruct((ROWS, QUERY_HEADS * HEAD_SIZE), BF16),
                jax.ShapeDtypeStruct((ROWS, kv_cols), BF16),
                jax.ShapeDtypeStruct((ROWS, kv_cols), BF16),
                jax.ShapeDtypeStruct((1, HEAD_SIZE), F32),
                jax.ShapeDtypeStruct((2, kv_cols), F32),
            ],
            in_specs=[any_space] * 4,
            out_specs=[any_space, vmem, vmem, vmem, vmem],
            scratch_shapes=[
                pltpu.VMEM((SLOTS, BLOCK, COLS), BF16),
                pltpu.VMEM((SLOTS, BLOCK, COLS), BF16),
                pltpu.VMEM((SLOTS, SPAN, HEAD_SIZE), BF16),
                pltpu.VMEM((SLOTS, SPAN, HEAD_SIZE), BF16),
                pltpu.VMEM((GROUP, SPAN, BLOCK), F32),
                pltpu.VMEM((GROUP, SPAN, BLOCK), F32),
                pltpu.VMEM((GROUP, HEAD_SIZE, BLOCK), F32),
                pltpu.VMEM((SLOTS, SPAN, HEAD_SIZE), BF16),
                pltpu.VMEM((SLOTS, SPAN, HEAD_SIZE), BF16),
                pltpu.VMEM((SLOTS, BLOCK, COLS), BF16),
                pltpu.VMEM((LINE + 1, ROWS, kv_cols), BF16),
                pltpu.VMEM((LINE + 1, ROWS, kv_cols), BF16),
                pltpu.VMEM((SLOTS, 2, LINE - 1, BLOCK, HEAD_SIZE), BF16),
                pltpu.VMEM((HALF, NOTE, 1, HEAD_SIZE), F32),
                pltpu.VMEM((MEMBERS, NOTE, 1, HEAD_SIZE), F32),
                pltpu.VMEM((2 * NOTE - 1, 1, HEAD_SIZE), F32),
                pltpu.VMEM((groups - 1, 2 * NOTE - 1, 1, HEAD_SIZE), F32),
                dma((KEYVALUE_HEADS, 2)),
                dma((SLOTS, 2)),
                dma((3, KEYVALUE_HEADS, 2)),
                dma((SLOTS, CHUNKS, 2)),
                dma((SLOTS, 2, LINE - 1, 2)),
                dma((SLOTS, CHUNKS, 2, 2)),
                dma((LINE + 1, 2)),
                dma((SLOTS, 2, LINE - 1)),
                dma((SLOTS, 2, LINE - 1)),
                dma((SLOTS, 2)),
                dma,
                dma((MEMBERS,)),
                dma,
                dma((groups - 1,)),
                dma,
            ],
            compiler_params=pltpu.CompilerParams(
                collective_id=0, has_side_effects=True, vmem_limit_bytes=60 * 2**20
            ),
            name="attention_grads",
        )(query_input, key_input, value_input, output_gradient)
    )
    return tuple(
        pl.pallas_call(
            hand_out,
            out_shape=[jax.ShapeDtypeStruct(x.shape, x.dtype) for x in results],
            in_specs=[vmem] * len(results),
            out_specs=[any_space] * len(results),
            scratch_shapes=[dma((len(results),))],
            name="hand_out",
        )(*results)
    )


def solution(mesh):
    rows = P(("dp", "seq"), None)
    return jax.shard_map(
        local,
        mesh=mesh,
        in_specs=(rows,) * 4,
        out_specs=(rows, rows, rows, P("seq", None), P()),
        check_vma=False,
    )
```
